256 devices in a mesh: lvl: 32 (over x, y, core), mid: 8 (over z).
Axes of the slice: x: 4, y: 4, z: 8, core: 2. Of those that a mesh axis runs over, the one named last changes fastest.
Arguments:
- signal: bfloat16 [8192, 64, 128], P(('lvl', 'mid')), may hold values from -6 to 6
- leaf_in: bfloat16 [8192, 64, 128], P(('lvl', 'mid')), may hold values from -0.5 to 0.5
- upper_w: bfloat16 [3, 8192, 64, 256], P(None, ('lvl', 'mid')), may hold values from -0.375 to 0.375
- middle_w: bfloat16 [2, 8192, 64, 256], P(None, ('lvl', 'mid')), may hold values from -0.375 to 0.375
- lower_w: bfloat16 [2, 8192, 64, 256], P(None, ('lvl', 'mid')), may hold values from -0.375 to 0.375
- leaf_out: bfloat16 [8192, 64, 128], P(('lvl', 'mid')), may hold values from -0.5 to 0.5
Outputs:
- applied: bfloat16 [8192, 64, 128], P(('lvl', 'mid'))
The draws below stay inside these ranges and needn't reach their ends.
All inputs are finite; a program needn't handle non-finite values.
Results may differ from the reference program's by a relative error of at most 0.018.
Values may be sent and summed in bfloat16 or wider, within the bound.
No kernel may reach another device: no remote copies, remote signals or barrier semaphores. Data moves between devices by JAX's collectives and lax.ppermute only.
A program may use at most 64 MiB of HBM per device.

```python
import jax
import jax.numpy as jnp
from jax import lax

RANK = 64
COLS = 128
BOX_DEV = 32
UPPER = 3
MIDDLE = 2
LOWER = 2
BOXES = 8192
N_LVL = 32
N_MID = 8


def shard_levels(key, shape, pieces, smallest, high):
    level = 1.0
    for axis_at, blocks in pieces:
        steps = jax.random.uniform(jax.random.fold_in(jax.random.fold_in(key, 6), axis_at), (blocks,), jnp.float32, smallest / len(pieces), high / len(pieces))
        level = level * jnp.repeat(jnp.exp(steps), shape[axis_at] // blocks).reshape((-1,) + (1,) * (len(shape) - 1 - axis_at))
    return level


def noise(key, shape, deviation, limit, split=(), dtype=jnp.bfloat16):
    drawn = jax.random.normal(key, shape, jnp.float32) * deviation
    if len(split) > 0:
        drawn = shard_levels(key, shape, split, -0.22, 0.18) * drawn
    return jnp.clip(drawn, min=-limit, max=limit).astype(dtype)


def setup_inputs(seed: int = 0) -> dict:
    seeds = jax.random.split(jax.random.key(seed), 7)
    signal = noise(seeds[0], (BOXES, RANK, COLS), 1.0, 6.0, ((0, 256),))
    leaf_in = noise(seeds[1], (BOXES, RANK, 2 * RANK), (2 * RANK) ** -0.5, 0.5, ((0, 256),))
    upper_w = noise(seeds[2], (UPPER, BOXES, RANK, 4 * RANK), (4 * RANK) ** -0.5, 0.375, ((1, 256),))
    middle_w = noise(seeds[3], (MIDDLE, BOXES, RANK, 4 * RANK), (4 * RANK) ** -0.5, 0.375, ((1, 256),))
    lower_w = noise(seeds[4], (LOWER, BOXES, RANK, 4 * RANK), (4 * RANK) ** -0.5, 0.375, ((1, 256),))
    leaf_out = noise(seeds[5], (BOXES, RANK, 2 * RANK), (2 * RANK) ** -0.5, 0.5, ((0, 256),))
    return dict(signal=signal, leaf_in=leaf_in, upper_w=upper_w, middle_w=middle_w, lower_w=lower_w, leaf_out=leaf_out)


def mix(weights, parts):
    boxes = weights.shape[0]
    rank_dim = weights.shape[1]
    shaped = weights.astype(jnp.float32).reshape(boxes, rank_dim, 2, len(parts), rank_dim)
    total = jnp.zeros((boxes, 2, rank_dim, parts[0].shape[-1]), jnp.float32)
    for s in range(len(parts)):
        total = total + jnp.einsum("nrak,nkc->narc", shaped[:, :, :, s, :], parts[s].astype(jnp.float32),
                                   precision=lax.Precision.HIGHEST)
    columns = total.shape[-1] // 2
    real_part = total[:, 0, :, :columns] - total[:, 1, :, columns:]
    imag_part = total[:, 0, :, columns:] + total[:, 1, :, :columns]
    return jnp.concatenate([real_part, imag_part], -1).astype(jnp.bfloat16)


def partner(field, outer, bit, inner):
    lead = field.shape[:-2]
    shaped = field.reshape((outer, -1, 2, inner) + field.shape[-2:])
    return jnp.flip(shaped, 2).reshape(lead + field.shape[-2:])


def grouped(array):
    return array.reshape((N_LVL, -1) + array.shape[1:])


def apply_level(weights, field, other):
    return lax.map(lambda items: mix(items[0], (items[1], items[2])), (grouped(weights), field, other))


def reference(signal, leaf_in, upper_w, middle_w, lower_w, leaf_out):
    field = lax.map(lambda items: mix(items[0], (items[1],)), (grouped(leaf_in), grouped(signal)))
    per_group = N_MID * BOX_DEV
    lvl_bits = N_LVL.bit_length() - 1
    mid_bits = N_MID.bit_length() - 1
    for step in range(UPPER):
        bit = lvl_bits - 1 - step
        other = partner(field, 1, bit, (1 << bit) * per_group)
        field = apply_level(upper_w[step], field, other)
    field = field.reshape(N_LVL, N_MID, N_MID, BOX_DEV // N_MID, RANK, COLS)
    field = jnp.swapaxes(field, 1, 2).reshape(N_LVL, per_group, RANK, COLS)
    for step in range(MIDDLE):
        bit = mid_bits - 1 - step
        other = partner(field, N_LVL * N_MID, bit, (1 << bit) * (BOX_DEV // N_MID))
        field = apply_level(middle_w[step], field, other)
    for step in range(LOWER):
        bit = LOWER - 1 - step
        other = partner(field, 1, bit, (1 << bit) * per_group)
        field = apply_level(lower_w[step], field, other)
    result = lax.map(lambda items: mix(items[0], (items[1],)), (grouped(leaf_out), field))
    return result.reshape(BOXES, RANK, COLS)
```

```python
import functools

import jax
import jax.numpy as jnp
from jax import lax
from jax.experimental import pallas as pl
from jax.experimental.pallas import tpu as pltpu
from jax.sharding import PartitionSpec as P

WIDTHS = (1, 1, 1, 1)
GROUPS = ((0, 1, 2, 3),)
LEAF_LIMIT = 8 << 20
PLAN = (
    "L0", "L1", "L2", "L3", "U00", "U01", "U02", "U10", "U03", "U11", "U20", "U12", "U21", "U13",
    "U22", "W0", "U23", "M0", "M1", "M2", "M3", "D00", "D01", "D02", "D03", "E012", "E3",
)
VMEM = pl.BlockSpec(memory_space=pltpu.VMEM)
ANY = pl.BlockSpec(memory_space=pl.ANY)
DMA = pltpu.SemaphoreType.DMA
TOKEN = jax.ShapeDtypeStruct((8, 128), jnp.float32)
COST = {"L": 0, "W": 0, "U0": 0, "U1": 0, "U2": 0, "M": 0, "D0": 0, "D1": 0}


def turn(piece):
    half = piece.shape[-1] // 2
    rolled = pltpu.roll(piece.astype(jnp.float32), half, 1)
    lane = lax.broadcasted_iota(jnp.int32, piece.shape, 1)
    return jnp.where(lane < half, -rolled, rolled).astype(jnp.bfloat16)


def product(weights, parts):
    stacked = jnp.concatenate(list(parts) + [turn(p) for p in parts], axis=0)
    return jnp.dot(weights, stacked, preferred_element_type=jnp.float32).astype(jnp.bfloat16)


def leaf_kernel(first, w_ref, x_ref, t_ref, o_ref, u_ref, ws_ref, xs_ref, sems):
    u_ref[...] = t_ref[...]
    width = o_ref.shape[1]
    loads = [
        pltpu.make_async_copy(w_ref.at[:, first:first + width], ws_ref, sems.at[0]),
        pltpu.make_async_copy(x_ref.at[:, first:first + width], xs_ref, sems.at[1]),
    ]
    for load in loads:
        load.start()
    for load in loads:
        load.wait()
    for a in range(o_ref.shape[0]):
        for b in range(width):
            o_ref[a, b] = product(ws_ref[a, b], [xs_ref[a, b]])


def stage_kernel(t_ref, *refs):
    count = (len(refs) - 2) // 2
    u_ref, sems = refs[-2:]
    u_ref[...] = t_ref[...]
    loads = [pltpu.make_async_copy(refs[i], refs[count + i], sems.at[i]) for i in range(count)]
    for load in loads:
        load.start()
    for load in loads:
        load.wait()


def level_kernel(first, step, w_ref, x_ref, y_ref, t_ref, o_ref, u_ref):
    u_ref[...] = t_ref[...]
    for a in range(o_ref.shape[0]):
        for b in range(o_ref.shape[1]):
            o_ref[a, b] = product(w_ref[step, a, first + b], [x_ref[a, b], y_ref[a, b]])


def join_kernel(first, step, w_ref, x_ref, y_ref, t_ref, *refs):
    *earlier, o_ref, u_ref, s_ref, sem = refs
    u_ref[...] = t_ref[...]
    at = 0
    stores = []
    for e_ref in earlier:
        stores.append(pltpu.make_async_copy(e_ref, o_ref.at[:, at:at + e_ref.shape[1]], sem))
        at += e_ref.shape[1]
    for a in range(s_ref.shape[0]):
        for b in range(x_ref.shape[1]):
            s_ref[a, b] = product(w_ref[step, a, first + b], [x_ref[a, b], y_ref[a, b]])
    stores.append(pltpu.make_async_copy(s_ref, o_ref.at[:, at:], sem))
    for store in stores:
        store.start()
    for store in stores:
        store.wait()


def middle_kernel(first, at, w_ref, x_ref, t_ref, o_ref, u_ref, x_scr, s_ref, sem):
    u_ref[...] = t_ref[...]
    count, width = o_ref.shape[:2]
    load = pltpu.make_async_copy(x_ref.at[:, at:at + width], x_scr, sem)
    load.start()
    load.wait()
    for a in range(count):
        for b in range(width):
            s_ref[a, b] = product(w_ref[0, a, first + b], [x_scr[a, b], x_scr[a ^ (count // 2), b]])
    for a in range(count):
        for b in range(width):
            o_ref[a, b] = product(w_ref[1, a, first + b], [s_ref[a, b], s_ref[a ^ (count // 4), b]])


def last_group_kernel(step, firsts, w_ref, v_ref, t_ref, *refs):
    o_ref, u_ref, r_ref, sems = refs[-4:]
    u_ref[...] = t_ref[...]
    stores = []
    for c, first in enumerate(firsts):
        x_ref, y_ref = refs[2 * c], refs[2 * c + 1]
        width = x_ref.shape[1]
        for a in range(x_ref.shape[0]):
            for b in range(width):
                value = product(w_ref[step, a, first + b], [x_ref[a, b], y_ref[a, b]])
                r_ref[a, first + b] = product(v_ref[a, first + b], [value])
        store = pltpu.make_async_copy(r_ref.at[:, first:first + width], o_ref.at[:, first:first + width], sems.at[c])
        store.start()
        stores.append(store)
    for store in stores:
        store.wait()


def call(kind, kernel, shapes, args, specs, out_specs, token, limit=8 << 20, **kw):
    *outs, token = pl.pallas_call(
        kernel,
        out_shape=[jax.ShapeDtypeStruct(shape, jnp.bfloat16) for shape in shapes] + [TOKEN],
        in_specs=specs,
        out_specs=list(out_specs) + [VMEM],
        compiler_params=pltpu.CompilerParams(vmem_limit_bytes=limit),
        cost_estimate=pl.CostEstimate(flops=1 + int(COST[kind] * 1e9), bytes_accessed=1, transcendentals=0),
        **kw,
    )(*args)
    return outs, token


def on_device(signal, leaf_in, upper_w, middle_w, lower_w, leaf_out):
    lvl_size, mid_size = lax.axis_size("lvl"), lax.axis_size("mid")
    lvl_bits = lvl_size.bit_length() - 1
    inner = signal.shape[0] // mid_size
    box = signal.shape[1:]
    part = functools.partial
    leaf_w, up_w, mid_w, low_w, out_w, samples = (
        v.reshape(v.shape[:-3] + (mid_size, inner) + v.shape[-2:])
        for v in (leaf_in, upper_w, middle_w, lower_w, leaf_out, signal)
    )
    firsts = [sum(WIDTHS[:c]) for c in range(len(WIDTHS))]
    shapes = [(mid_size, w) + box for w in WIDTHS]

    def swap(block, bit):
        return lax.ppermute(block, "lvl", [(i, i ^ (1 << bit)) for i in range(lvl_size)])

    field, other, place = {}, {}, {}
    token = jnp.zeros(TOKEN.shape, TOKEN.dtype)
    result = None
    lower_count = lower_w.shape[0]
    upper_count = upper_w.shape[0]
    for item in PLAN:
        kind, c = item[0], int(item[-1])
        step = int(item[1])
        name = item[:-1] if kind in "UD" else kind
        name = name if item not in COST else item
        first, shape = firsts[c], shapes[c]
        block = pltpu.VMEM(shape, jnp.bfloat16)
        if kind == "W":
            staged = (mid_w, low_w, out_w)
            (mid_w, low_w, out_w), token = call(name, stage_kernel, [v.shape for v in staged], (token, *staged),
                                                      [VMEM] + [ANY] * 3, [VMEM] * 3, token, scratch_shapes=[DMA((3,))])
        elif kind == "L":
            (field[c],), token = call(name, part(leaf_kernel, first), [shape], (leaf_w, samples, token), [ANY, ANY, VMEM],
                                      [VMEM], token, LEAF_LIMIT if c == 0 else 8 << 20,
                                      scratch_shapes=[block, block, DMA((2,))])
            other[c] = swap(field[c], lvl_bits - 1)
        elif kind == "U" and (step < upper_count - 1 or c not in [g[-1] for g in GROUPS]):
            (field[c],), token = call(name, part(level_kernel, first, step), [shape], (up_w, field[c], other[c], token),
                                      [VMEM] * 4, [VMEM], token)
            if step < upper_count - 1:
                other[c] = swap(field[c], lvl_bits - 2 - step)
        elif kind == "U":
            group = next(g for g in GROUPS if c in g)
            earlier = [field[e] for e in group[:-1]]
            whole = (mid_size, sum(WIDTHS[e] for e in group)) + box
            (joined,), token = call(name, part(join_kernel, first, step), [whole],
                                    (up_w, field[c], other[c], token, *earlier), [VMEM] * (4 + len(earlier)), [ANY],
                                    token, scratch_shapes=[block, DMA])
            moved = lax.all_to_all(joined, "mid", split_axis=0, concat_axis=0, tiled=True)
            at = 0
            for e in group:
                field[e], place[e] = moved, at
                at += WIDTHS[e]
        elif kind == "M":
            (field[c],), token = call(name, part(middle_kernel, first, place[c]), [shape], (mid_w, field[c], token),
                                      [VMEM, ANY, VMEM], [VMEM], token, scratch_shapes=[block, block, DMA])
            other[c] = swap(field[c], lower_count - 1)
        elif kind == "D" and step < lower_count - 1:
            (field[c],), token = call(name, part(level_kernel, first, step), [shape], (low_w, field[c], other[c], token),
                                      [VMEM] * 4, [VMEM], token)
            other[c] = swap(field[c], lower_count - 2 - step)
        elif kind == "E":
            chosen = [int(e) for e in item[1:]]
            pairs = [v for e in chosen for v in (field[e], other[e])]
            args, specs, alias = (low_w, out_w, token, *pairs), [VMEM] * (3 + len(pairs)), {}
            if result is not None:
                args, specs, alias = args + (result,), specs + [ANY], {len(args): 0}
            (result,), token = call("D1", part(last_group_kernel, lower_count - 1, [firsts[e] for e in chosen]),
                                    [samples.shape], args, specs, [ANY], token, input_output_aliases=alias,
                                    scratch_shapes=[pltpu.VMEM(samples.shape, jnp.bfloat16), DMA((len(chosen),))])
    return result.reshape(signal.shape)


def solution(mesh):
    boxes = P(("lvl", "mid"), None, None)
    levels = P(None, ("lvl", "mid"), None, None)
    return jax.shard_map(
        on_device,
        mesh=mesh,
        in_specs=(boxes, boxes, levels, levels, levels, boxes),
        out_specs=boxes,
        check_vma=False,
    )
```

```python
import functools

import jax
import jax.numpy as jnp
from jax import lax
from jax.experimental import pallas as pl
from jax.experimental.pallas import tpu as pltpu
from jax.sharding import PartitionSpec as P

WIDTHS = (1, 1, 1, 1)
GROUPS = ((0, 1, 2, 3),)
LEAF_LIMIT = 8 << 20
PLAN = (
    "T0", "L0", "L1", "L2", "L3", "U00", "U01", "U02", "U03", "U10", "U11", "U12", "U13", "U20", "U21",
    "U22", "W0", "U23", "M0", "M1", "M2", "M3", "D00", "D01", "D02", "D03", "E012", "E3",
)
VMEM = pl.BlockSpec(memory_space=pltpu.VMEM)
ANY = pl.BlockSpec(memory_space=pl.ANY)
DMA = pltpu.SemaphoreType.DMA
TOKEN = jax.ShapeDtypeStruct((8, 128), jnp.float32)
COST = {"T0": 100}


def turn(piece):
    half = piece.shape[-1] // 2
    rolled = pltpu.roll(piece.astype(jnp.float32), half, 1)
    lane = lax.broadcasted_iota(jnp.int32, piece.shape, 1)
    return jnp.where(lane < half, -rolled, rolled).astype(jnp.bfloat16)


def product(weights, parts):
    stacked = jnp.concatenate(list(parts) + [turn(p) for p in parts], axis=0)
    return jnp.dot(weights, stacked, preferred_element_type=jnp.float32).astype(jnp.bfloat16)


def token_kernel(t_ref, u_ref):
    u_ref[...] = t_ref[...]


def leaf_kernel(first, w_ref, x_ref, t_ref, o_ref, u_ref, ws_ref, xs_ref, sems):
    u_ref[...] = t_ref[...]
    width = o_ref.shape[1]
    loads = [
        pltpu.make_async_copy(w_ref.at[:, first:first + width], ws_ref, sems.at[0]),
        pltpu.make_async_copy(x_ref.at[:, first:first + width], xs_ref, sems.at[1]),
    ]
    for load in loads:
        load.start()
    for load in loads:
        load.wait()
    for a in range(o_ref.shape[0]):
        for b in range(width):
            o_ref[a, b] = product(ws_ref[a, b], [xs_ref[a, b]])


def stage_kernel(t_ref, *refs):
    count = (len(refs) - 2) // 2
    u_ref, sems = refs[-2:]
    u_ref[...] = t_ref[...]
    loads = [pltpu.make_async_copy(refs[i], refs[count + i], sems.at[i]) for i in range(count)]
    for load in loads:
        load.start()
    for load in loads:
        load.wait()


def level_kernel(first, step, w_ref, x_ref, y_ref, t_ref, o_ref, u_ref):
    u_ref[...] = t_ref[...]
    for a in range(o_ref.shape[0]):
        for b in range(o_ref.shape[1]):
            o_ref[a, b] = product(w_ref[step, a, first + b], [x_ref[a, b], y_ref[a, b]])


def join_kernel(first, step, w_ref, x_ref, y_ref, t_ref, *refs):
    *earlier, o_ref, u_ref, s_ref, sem = refs
    u_ref[...] = t_ref[...]
    at = 0
    stores = []
    for e_ref in earlier:
        stores.append(pltpu.make_async_copy(e_ref, o_ref.at[:, at:at + e_ref.shape[1]], sem))
        at += e_ref.shape[1]
    for a in range(s_ref.shape[0]):
        for b in range(x_ref.shape[1]):
            s_ref[a, b] = product(w_ref[step, a, first + b], [x_ref[a, b], y_ref[a, b]])
    stores.append(pltpu.make_async_copy(s_ref, o_ref.at[:, at:], sem))
    for store in stores:
        store.start()
    for store in stores:
        store.wait()


def middle_kernel(first, at, w_ref, x_ref, t_ref, o_ref, u_ref, x_scr, s_ref, sem):
    u_ref[...] = t_ref[...]
    count, width = o_ref.shape[:2]
    load = pltpu.make_async_copy(x_ref.at[:, at:at + width], x_scr, sem)
    load.start()
    load.wait()
    for a in range(count):
        for b in range(width):
            s_ref[a, b] = product(w_ref[0, a, first + b], [x_scr[a, b], x_scr[a ^ (count // 2), b]])
    for a in range(count):
        for b in range(width):
            o_ref[a, b] = product(w_ref[1, a, first + b], [s_ref[a, b], s_ref[a ^ (count // 4), b]])


def finish(step, first, w_ref, v_ref, x_ref, y_ref, r_ref, at):
    for a in range(x_ref.shape[0]):
        for b in range(x_ref.shape[1]):
            value = product(w_ref[step, a, first + b], [x_ref[a, b], y_ref[a, b]])
            r_ref[a, at + b] = product(v_ref[a, first + b], [value])


def finish_kernel(step, firsts, w_ref, v_ref, t_ref, *refs):
    r_ref, u_ref = refs[-2:]
    u_ref[...] = t_ref[...]
    for c, first in enumerate(firsts):
        finish(step, first, w_ref, v_ref, refs[2 * c], refs[2 * c + 1], r_ref, first - firsts[0])


def store_kernel(step, first, w_ref, v_ref, t_ref, x_ref, y_ref, *refs):
    *earlier, o_ref, r_ref, sems = refs
    stores = []
    at = 0
    for e_ref in earlier:
        stores.append(pltpu.make_async_copy(e_ref, o_ref.at[:, at:at + e_ref.shape[1]], sems.at[len(stores)]))
        at += e_ref.shape[1]
    for store in stores:
        store.start()
    finish(step, first, w_ref, v_ref, x_ref, y_ref, r_ref, 0)
    stores.append(pltpu.make_async_copy(r_ref, o_ref.at[:, first:first + x_ref.shape[1]], sems.at[len(stores)]))
    stores[-1].start()
    for store in stores:
        store.wait()


def call(kind, kernel, shapes, args, specs, out_specs, token, limit=8 << 20, **kw):
    *outs, token = pl.pallas_call(
        kernel,
        out_shape=[jax.ShapeDtypeStruct(shape, jnp.bfloat16) for shape in shapes] + [TOKEN],
        in_specs=specs,
        out_specs=list(out_specs) + [VMEM],
        compiler_params=pltpu.CompilerParams(vmem_limit_bytes=limit),
        cost_estimate=pl.CostEstimate(flops=1 + int(COST.get(kind, 0) * 1e9), bytes_accessed=1, transcendentals=0),
        **kw,
    )(*args)
    return outs, token


def on_device(signal, leaf_in, upper_w, middle_w, lower_w, leaf_out):
    lvl_size, mid_size = lax.axis_size("lvl"), lax.axis_size("mid")
    lvl_bits = lvl_size.bit_length() - 1
    inner = signal.shape[0] // mid_size
    box = signal.shape[1:]
    part = functools.partial
    leaf_w, up_w, mid_w, low_w, out_w, samples = (
        v.reshape(v.shape[:-3] + (mid_size, inner) + v.shape[-2:])
        for v in (leaf_in, upper_w, middle_w, lower_w, leaf_out, signal)
    )
    firsts = [sum(WIDTHS[:c]) for c in range(len(WIDTHS))]
    shapes = [(mid_size, w) + box for w in WIDTHS]

    def swap(block, bit):
        return lax.ppermute(block, "lvl", [(i, i ^ (1 << bit)) for i in range(lvl_size)])

    field, other, place = {}, {}, {}
    token = jnp.zeros(TOKEN.shape, TOKEN.dtype)
    result, finished = None, []
    lower_count = lower_w.shape[0]
    upper_count = upper_w.shape[0]
    for item in PLAN:
        kind, c = item[0], int(item[-1])
        step = int(item[1])
        name = item
        first, shape = firsts[c], shapes[c]
        block = pltpu.VMEM(shape, jnp.bfloat16)
        if kind == "T":
            _, token = call(name, token_kernel, [], (token,), [VMEM], [], token)
        elif kind == "W":
            staged = (mid_w, low_w, out_w)
            (mid_w, low_w, out_w), token = call(name, stage_kernel, [v.shape for v in staged], (token, *staged),
                                                      [VMEM] + [ANY] * 3, [VMEM] * 3, token, scratch_shapes=[DMA((3,))])
        elif kind == "L":
            (field[c],), token = call(name, part(leaf_kernel, first), [shape], (leaf_w, samples, token), [ANY, ANY, VMEM],
                                      [VMEM], token, LEAF_LIMIT if c == 0 else 8 << 20,
                                      scratch_shapes=[block, block, DMA((2,))])
            other[c] = swap(field[c], lvl_bits - 1)
        elif kind == "U" and (step < upper_count - 1 or c not in [g[-1] for g in GROUPS]):
            (field[c],), token = call(name, part(level_kernel, first, step), [shape], (up_w, field[c], other[c], token),
                                      [VMEM] * 4, [VMEM], token)
            if step < upper_count - 1:
                other[c] = swap(field[c], lvl_bits - 2 - step)
        elif kind == "U":
            group = next(g for g in GROUPS if c in g)
            earlier = [field[e] for e in group[:-1]]
            whole = (mid_size, sum(WIDTHS[e] for e in group)) + box
            (joined,), token = call(name, part(join_kernel, first, step), [whole],
                                    (up_w, field[c], other[c], token, *earlier), [VMEM] * (4 + len(earlier)), [ANY],
                                    token, scratch_shapes=[block, DMA])
            moved = lax.all_to_all(joined, "mid", split_axis=0, concat_axis=0, tiled=True)
            at = 0
            for e in group:
                field[e], place[e] = moved, at
                at += WIDTHS[e]
        elif kind == "M":
            (field[c],), token = call(name, part(middle_kernel, first, place[c]), [shape], (mid_w, field[c], token),
                                      [VMEM, ANY, VMEM], [VMEM], token, scratch_shapes=[block, block, DMA])
            other[c] = swap(field[c], lower_count - 1)
        elif kind == "D" and step < lower_count - 1:
            (field[c],), token = call(name, part(level_kernel, first, step), [shape], (low_w, field[c], other[c], token),
                                      [VMEM] * 4, [VMEM], token)
            other[c] = swap(field[c], lower_count - 2 - step)
        elif kind == "E" and item != PLAN[-1]:
            chosen = [int(e) for e in item[1:]]
            pairs = [v for e in chosen for v in (field[e], other[e])]
            whole = (mid_size, sum(WIDTHS[e] for e in chosen)) + box
            (done,), token = call(name, part(finish_kernel, lower_count - 1, [firsts[e] for e in chosen]), [whole],
                                  (low_w, out_w, token, *pairs), [VMEM] * (3 + len(pairs)), [VMEM], token)
            finished.append(done)
        elif kind == "E":
            args = (low_w, out_w, token, field[c], other[c], *finished)
            result = pl.pallas_call(
                part(store_kernel, lower_count - 1, first),
                out_shape=jax.ShapeDtypeStruct(samples.shape, jnp.bfloat16),
                in_specs=[VMEM] * len(args),
                out_specs=ANY,
                scratch_shapes=[block, DMA((1 + len(finished),))],
                compiler_params=pltpu.CompilerParams(vmem_limit_bytes=8 << 20),
                cost_estimate=pl.CostEstimate(flops=1, bytes_accessed=1, transcendentals=0),
            )(*args)
    return result.reshape(signal.shape)


def solution(mesh):
    boxes = P(("lvl", "mid"), None, None)
    levels = P(None, ("lvl", "mid"), None, None)
    return jax.shard_map(
        on_device,
        mesh=mesh,
        in_specs=(boxes, boxes, levels, levels, levels, boxes),
        out_specs=boxes,
        check_vma=False,
    )
```

```python
import functools

import jax
import jax.numpy as jnp
from jax import lax
from jax.experimental import pallas as pl
from jax.experimental.pallas import tpu as pltpu
from jax.sharding import PartitionSpec as P

WIDTHS = (1, 1, 1, 1)
PIECES = 1
PLAN = (
    "T0", "L0", "L1", "L2", "L3", "U00", "U01", "U02", "U03", "U10", "U11", "U12", "U13", "U20", "U21",
    "U22", "W0", "U23", "M0", "M1", "D00", "D01", "E0", "E1",
)
VMEM = pl.BlockSpec(memory_space=pltpu.VMEM)
ANY = pl.BlockSpec(memory_space=pl.ANY)
DMA = pltpu.SemaphoreType.DMA
TOKEN = jax.ShapeDtypeStruct((8, 128), jnp.float32)
COST = {"T0": 100}


def turn(piece):
    half = piece.shape[-1] // 2
    rolled = pltpu.roll(piece.astype(jnp.float32), half, 1)
    lane = lax.broadcasted_iota(jnp.int32, piece.shape, 1)
    return jnp.where(lane < half, -rolled, rolled).astype(jnp.bfloat16)


def product(weights, parts):
    stacked = jnp.concatenate(list(parts) + [turn(p) for p in parts], axis=0)
    return jnp.dot(weights, stacked, preferred_element_type=jnp.float32).astype(jnp.bfloat16)


def token_kernel(t_ref, u_ref):
    u_ref[...] = t_ref[...]


def leaf_kernel(first, w_ref, x_ref, t_ref, o_ref, u_ref, ws_ref, xs_ref, sems):
    u_ref[...] = t_ref[...]
    width = o_ref.shape[1]
    loads = [
        pltpu.make_async_copy(w_ref.at[:, first:first + width], ws_ref, sems.at[0]),
        pltpu.make_async_copy(x_ref.at[:, first:first + width], xs_ref, sems.at[1]),
    ]
    for load in loads:
        load.start()
    for load in loads:
        load.wait()
    for a in range(o_ref.shape[0]):
        for b in range(width):
            o_ref[a, b] = product(ws_ref[a, b], [xs_ref[a, b]])


def stage_kernel(t_ref, *refs):
    count = (len(refs) - 2) // 2
    u_ref, sems = refs[-2:]
    u_ref[...] = t_ref[...]
    loads = [pltpu.make_async_copy(refs[i], refs[count + i], sems.at[i]) for i in range(count)]
    for load in loads:
        load.start()
    for load in loads:
        load.wait()


def level_kernel(first, step, w_ref, x_ref, y_ref, t_ref, o_ref, u_ref):
    u_ref[...] = t_ref[...]
    for a in range(o_ref.shape[0]):
        for b in range(o_ref.shape[1]):
            o_ref[a, b] = product(w_ref[step, a, first + b], [x_ref[a, b], y_ref[a, b]])


def spread_kernel(first, step, w_ref, x_ref, y_ref, t_ref, *refs):
    *earlier, u_ref = refs
    count = x_ref.shape[0]
    earlier, outs = earlier[:-count], earlier[-count:]
    u_ref[...] = t_ref[...]
    me = lax.axis_index("mid")
    for q in range(count):
        a = me ^ q
        at = 0
        for e_ref in earlier:
            outs[q][at:at + e_ref.shape[1]] = e_ref[a]
            at += e_ref.shape[1]
        for b in range(x_ref.shape[1]):
            outs[q][at + b] = product(w_ref[step, a, first + b], [x_ref[a, b], y_ref[a, b]])


def middle_kernel(gaps, w_ref, t_ref, *refs):
    count = len(gaps)
    got, outs, u_ref, s_ref = refs[:count], refs[count:-2], refs[-2], refs[-1]
    u_ref[...] = t_ref[...]
    me = lax.axis_index("mid")
    width = outs[0].shape[1]
    for i, q in enumerate(gaps):
        for b in range(s_ref.shape[1]):
            s_ref[i, b] = product(w_ref[0, me ^ q, b], [got[i][b], got[i ^ (count // 2)][b]])
    for i, q in enumerate(gaps):
        for b in range(s_ref.shape[1]):
            outs[b // width][i, b % width] = product(w_ref[1, me ^ q, b], [s_ref[i, b], s_ref[i ^ (count // 4), b]])


def lower_kernel(gaps, first, step, w_ref, x_ref, y_ref, t_ref, o_ref, u_ref):
    u_ref[...] = t_ref[...]
    me = lax.axis_index("mid")
    for i, q in enumerate(gaps):
        for b in range(o_ref.shape[1]):
            o_ref[i, b] = product(w_ref[step, me ^ q, first + b], [x_ref[i, b], y_ref[i, b]])


def finish(gaps, first, step, w_ref, v_ref, x_ref, y_ref, r_ref):
    me = lax.axis_index("mid")
    for i, q in enumerate(gaps):
        for b in range(x_ref.shape[1]):
            value = product(w_ref[step, me ^ q, first + b], [x_ref[i, b], y_ref[i, b]])
            r_ref[i, b] = product(v_ref[me ^ q, first + b], [value])


def finish_kernel(gaps, first, step, w_ref, v_ref, t_ref, x_ref, y_ref, r_ref, u_ref):
    u_ref[...] = t_ref[...]
    finish(gaps, first, step, w_ref, v_ref, x_ref, y_ref, r_ref)


def store_kernel(places, step, w_ref, v_ref, t_ref, x_ref, y_ref, *refs):
    *earlier, o_ref, r_ref, sems = refs
    me = lax.axis_index("mid")
    width = r_ref.shape[1]

    def stores(c, source):
        gaps, first = places[c]
        return [
            pltpu.make_async_copy(source.at[i], o_ref.at[me ^ q, first:first + width], sems.at[c * len(gaps) + i])
            for i, q in enumerate(gaps)
        ]

    moving = [store for c, e_ref in enumerate(earlier) for store in stores(c, e_ref)]
    for store in moving:
        store.start()
    gaps, first = places[-1]
    finish(gaps, first, step, w_ref, v_ref, x_ref, y_ref, r_ref)
    final = stores(len(places) - 1, r_ref)
    for store in final:
        store.start()
    for store in moving + final:
        store.wait()


def call(kind, kernel, shapes, args, specs, out_specs, token, **kw):
    *outs, token = pl.pallas_call(
        kernel,
        out_shape=[jax.ShapeDtypeStruct(shape, jnp.bfloat16) for shape in shapes] + [TOKEN],
        in_specs=specs,
        out_specs=list(out_specs) + [VMEM],
        compiler_params=pltpu.CompilerParams(vmem_limit_bytes=8 << 20),
        cost_estimate=pl.CostEstimate(flops=1 + int(COST.get(kind, 0) * 1e9), bytes_accessed=1, transcendentals=0),
        **kw,
    )(*args)
    return outs, token


def on_device(signal, leaf_in, upper_w, middle_w, lower_w, leaf_out):
    lvl_size, mid_size = lax.axis_size("lvl"), lax.axis_size("mid")
    lvl_bits = lvl_size.bit_length() - 1
    inner = signal.shape[0] // mid_size
    box = signal.shape[1:]
    part = functools.partial
    leaf_w, up_w, mid_w, low_w, out_w, samples = (
        v.reshape(v.shape[:-3] + (mid_size, inner) + v.shape[-2:])
        for v in (leaf_in, upper_w, middle_w, lower_w, leaf_out, signal)
    )
    firsts = [sum(WIDTHS[:c]) for c in range(len(WIDTHS))]
    shapes = [(mid_size, w) + box for w in WIDTHS]

    def swap(block, bit):
        return lax.ppermute(block, "lvl", [(i, i ^ (1 << bit)) for i in range(lvl_size)])

    def across(block, gap):
        return lax.ppermute(block, "mid", [(i, i ^ gap) for i in range(mid_size)])

    field, other, place = {}, {}, {}
    token = jnp.zeros(TOKEN.shape, TOKEN.dtype)
    result, finished = None, []
    lower_count = lower_w.shape[0]
    upper_count = upper_w.shape[0]
    for item in PLAN:
        kind, c = item[0], int(item[-1])
        step = int(item[1])
        name = item
        first, shape = firsts[c], shapes[c]
        block = pltpu.VMEM(shape, jnp.bfloat16)
        if kind == "T":
            _, token = call(name, token_kernel, [], (token,), [VMEM], [], token)
        elif kind == "W":
            staged = (mid_w, low_w, out_w)
            (mid_w, low_w, out_w), token = call(name, stage_kernel, [v.shape for v in staged], (token, *staged),
                                                      [VMEM] + [ANY] * 3, [VMEM] * 3, token, scratch_shapes=[DMA((3,))])
        elif kind == "L":
            (field[c],), token = call(name, part(leaf_kernel, first), [shape], (leaf_w, samples, token), [ANY, ANY, VMEM],
                                      [VMEM], token,
                                      scratch_shapes=[block, block, DMA((2,))])
            other[c] = swap(field[c], lvl_bits - 1)
        elif kind == "U" and (step < upper_count - 1 or c < len(WIDTHS) - 1):
            (field[c],), token = call(name, part(level_kernel, first, step), [shape], (up_w, field[c], other[c], token),
                                      [VMEM] * 4, [VMEM], token)
            if step < upper_count - 1:
                other[c] = swap(field[c], lvl_bits - 2 - step)
        elif kind == "U":
            earlier = [field[e] for e in range(c)]
            sends, token = call(name, part(spread_kernel, first, step), [(inner,) + box] * mid_size,
                                (up_w, field[c], other[c], token, *earlier), [VMEM] * (4 + len(earlier)),
                                [VMEM] * mid_size, token)
            got = [across(send, gap) if gap else send for gap, send in enumerate(sends)]
        elif kind == "M":
            gaps = tuple(range(c, mid_size, 2))
            tall = (len(gaps), inner)
            fields, token = call(name, part(middle_kernel, gaps), [(len(gaps), inner // PIECES) + box] * PIECES,
                                 (mid_w, token, *[got[q] for q in gaps]), [VMEM] * (2 + len(gaps)), [VMEM] * PIECES,
                                 token, scratch_shapes=[pltpu.VMEM(tall + box, jnp.bfloat16)])
            for piece, value in enumerate(fields):
                e = c * PIECES + piece
                field[e], other[e] = value, swap(value, lower_count - 1)
                place[e] = (gaps, piece * (inner // PIECES))
        elif kind == "D":
            (field[c],), token = call(name, part(lower_kernel, *place[c], step), [field[c].shape],
                                      (low_w, field[c], other[c], token), [VMEM] * 4, [VMEM], token)
            other[c] = swap(field[c], lower_count - 2 - step)
        elif item != PLAN[-1]:
            (done,), token = call(name, part(finish_kernel, *place[c], lower_count - 1), [field[c].shape],
                                  (low_w, out_w, token, field[c], other[c]), [VMEM] * 5, [VMEM], token)
            finished.append(done)
        else:
            args = (low_w, out_w, token, field[c], other[c], *finished)
            places = [place[e] for e in range(c + 1)]
            result = pl.pallas_call(
                part(store_kernel, places, lower_count - 1),
                out_shape=jax.ShapeDtypeStruct(samples.shape, jnp.bfloat16),
                in_specs=[VMEM] * len(args),
                out_specs=ANY,
                scratch_shapes=[pltpu.VMEM(field[c].shape, jnp.bfloat16), DMA((mid_size * PIECES,))],
                compiler_params=pltpu.CompilerParams(vmem_limit_bytes=8 << 20),
                cost_estimate=pl.CostEstimate(flops=1, bytes_accessed=1, transcendentals=0),
            )(*args)
    return result.reshape(signal.shape)


def solution(mesh):
    boxes = P(("lvl", "mid"), None, None)
    levels = P(None, ("lvl", "mid"), None, None)
    return jax.shard_map(
        on_device,
        mesh=mesh,
        in_specs=(boxes, boxes, levels, levels, levels, boxes),
        out_specs=boxes,
        check_vma=False,
    )
```

```python
import functools

import jax
import jax.numpy as jnp
from jax import lax
from jax.experimental import pallas as pl
from jax.experimental.pallas import tpu as pltpu
from jax.sharding import PartitionSpec as P

WIDTHS = (1, 1, 1, 1)
PIECES = (1, 1)
ORDER = ((0, 4, 6, 2), (7, 5, 1, 3))
PLAN = (
    "T0", "L0", "L1", "L2", "L3", "U00", "U01", "U02", "U03", "U10", "U11", "U12", "U13", "U20", "U21",
    "W0", "U22", "U23", "M0", "M1", "D00", "D01", "E0", "E1",
)
VMEM = pl.BlockSpec(memory_space=pltpu.VMEM)
ANY = pl.BlockSpec(memory_space=pl.ANY)
DMA = pltpu.SemaphoreType.DMA
TOKEN = jax.ShapeDtypeStruct((8, 128), jnp.float32)
COST = {"T0": 100}


def turn(piece):
    half = piece.shape[-1] // 2
    rolled = pltpu.roll(piece.astype(jnp.float32), half, 1)
    lane = lax.broadcasted_iota(jnp.int32, piece.shape, 1)
    return jnp.where(lane < half, -rolled, rolled).astype(jnp.bfloat16)


def product(weights, parts):
    stacked = jnp.concatenate(list(parts) + [turn(p) for p in parts], axis=0)
    return jnp.dot(weights, stacked, preferred_element_type=jnp.float32).astype(jnp.bfloat16)


def token_kernel(t_ref, u_ref):
    u_ref[...] = t_ref[...]


def leaf_kernel(first, w_ref, x_ref, t_ref, o_ref, u_ref, ws_ref, xs_ref, sems):
    u_ref[...] = t_ref[...]
    width = o_ref.shape[1]
    loads = [
        pltpu.make_async_copy(w_ref.at[:, first:first + width], ws_ref, sems.at[0]),
        pltpu.make_async_copy(x_ref.at[:, first:first + width], xs_ref, sems.at[1]),
    ]
    for load in loads:
        load.start()
    for load in loads:
        load.wait()
    for a in range(o_ref.shape[0]):
        for b in range(width):
            o_ref[a, b] = product(ws_ref[a, b], [xs_ref[a, b]])


def stage_kernel(t_ref, *refs):
    count = (len(refs) - 2) // 2
    u_ref, sems = refs[-2:]
    u_ref[...] = t_ref[...]
    loads = [pltpu.make_async_copy(refs[i], refs[count + i], sems.at[i]) for i in range(count)]
    for load in loads:
        load.start()
    for load in loads:
        load.wait()


def level_kernel(first, step, w_ref, x_ref, y_ref, t_ref, o_ref, u_ref):
    u_ref[...] = t_ref[...]
    for a in range(o_ref.shape[0]):
        for b in range(o_ref.shape[1]):
            o_ref[a, b] = product(w_ref[step, a, first + b], [x_ref[a, b], y_ref[a, b]])


def spread_kernel(first, step, w_ref, x_ref, y_ref, t_ref, *refs):
    *earlier, u_ref = refs
    count = x_ref.shape[0]
    earlier, outs = earlier[:-count], earlier[-count:]
    u_ref[...] = t_ref[...]
    me = lax.axis_index("mid")
    for q in range(count):
        a = me ^ q
        at = 0
        for e_ref in earlier:
            outs[q][at:at + e_ref.shape[1]] = e_ref[a]
            at += e_ref.shape[1]
        for b in range(x_ref.shape[1]):
            outs[q][at + b] = product(w_ref[step, a, first + b], [x_ref[a, b], y_ref[a, b]])


def middle_kernel(gaps, order, w_ref, t_ref, *refs):
    count = len(gaps)
    got = [refs[order.index(q)] for q in gaps]
    outs, u_ref, s_ref = refs[count:-2], refs[-2], refs[-1]
    u_ref[...] = t_ref[...]
    me = lax.axis_index("mid")
    width = outs[0].shape[1]
    for i, q in enumerate(gaps):
        for b in range(s_ref.shape[1]):
            s_ref[i, b] = product(w_ref[0, me ^ q, b], [got[i][b], got[i ^ (count // 2)][b]])
    for i, q in enumerate(gaps):
        for b in range(s_ref.shape[1]):
            outs[b // width][i, b % width] = product(w_ref[1, me ^ q, b], [s_ref[i, b], s_ref[i ^ (count // 4), b]])


def lower_kernel(gaps, first, step, w_ref, x_ref, y_ref, t_ref, o_ref, u_ref):
    u_ref[...] = t_ref[...]
    me = lax.axis_index("mid")
    for i, q in enumerate(gaps):
        for b in range(o_ref.shape[1]):
            o_ref[i, b] = product(w_ref[step, me ^ q, first + b], [x_ref[i, b], y_ref[i, b]])


def finish(gaps, first, step, w_ref, v_ref, x_ref, y_ref, r_ref):
    me = lax.axis_index("mid")
    for i, q in enumerate(gaps):
        for b in range(x_ref.shape[1]):
            value = product(w_ref[step, me ^ q, first + b], [x_ref[i, b], y_ref[i, b]])
            r_ref[i, b] = product(v_ref[me ^ q, first + b], [value])


def finish_kernel(gaps, first, step, w_ref, v_ref, t_ref, x_ref, y_ref, r_ref, u_ref):
    u_ref[...] = t_ref[...]
    finish(gaps, first, step, w_ref, v_ref, x_ref, y_ref, r_ref)


def store_kernel(places, step, w_ref, v_ref, t_ref, x_ref, y_ref, *refs):
    *earlier, o_ref, r_ref, sems = refs
    me = lax.axis_index("mid")

    def stores(c, source):
        gaps, first = places[c]
        width = source.shape[1]
        return [
            pltpu.make_async_copy(source.at[i], o_ref.at[me ^ q, first:first + width], sems.at[c * len(gaps) + i])
            for i, q in enumerate(gaps)
        ]

    moving = [store for c, e_ref in enumerate(earlier) for store in stores(c, e_ref)]
    for store in moving:
        store.start()
    gaps, first = places[-1]
    final = stores(len(places) - 1, r_ref)
    for i, q in enumerate(gaps):
        for b in range(x_ref.shape[1]):
            value = product(w_ref[step, me ^ q, first + b], [x_ref[i, b], y_ref[i, b]])
            r_ref[i, b] = product(v_ref[me ^ q, first + b], [value])
        final[i].start()
    for store in moving + final:
        store.wait()


def call(kind, kernel, shapes, args, specs, out_specs, token, **kw):
    *outs, token = pl.pallas_call(
        kernel,
        out_shape=[jax.ShapeDtypeStruct(shape, jnp.bfloat16) for shape in shapes] + [TOKEN],
        in_specs=specs,
        out_specs=list(out_specs) + [VMEM],
        compiler_params=pltpu.CompilerParams(vmem_limit_bytes=8 << 20),
        cost_estimate=pl.CostEstimate(flops=1 + int(COST.get(kind, 0) * 1e9), bytes_accessed=1, transcendentals=0),
        **kw,
    )(*args)
    return outs, token


def on_device(signal, leaf_in, upper_w, middle_w, lower_w, leaf_out):
    lvl_size, mid_size = lax.axis_size("lvl"), lax.axis_size("mid")
    lvl_bits = lvl_size.bit_length() - 1
    inner = signal.shape[0] // mid_size
    box = signal.shape[1:]
    part = functools.partial
    leaf_w, up_w, mid_w, low_w, out_w, samples = (
        v.reshape(v.shape[:-3] + (mid_size, inner) + v.shape[-2:])
        for v in (leaf_in, upper_w, middle_w, lower_w, leaf_out, signal)
    )
    firsts = [sum(WIDTHS[:c]) for c in range(len(WIDTHS))]
    shapes = [(mid_size, w) + box for w in WIDTHS]

    def swap(block, bit):
        return lax.ppermute(block, "lvl", [(i, i ^ (1 << bit)) for i in range(lvl_size)])

    def across(block, gap):
        return lax.ppermute(block, "mid", [(i, i ^ gap) for i in range(mid_size)])

    field, other, place = {}, {}, {}
    token = jnp.zeros(TOKEN.shape, TOKEN.dtype)
    result, finished = None, []
    lower_count = lower_w.shape[0]
    upper_count = upper_w.shape[0]
    for item in PLAN:
        kind, c = item[0], int(item[-1])
        step = int(item[1])
        name = item
        first, shape = firsts[c], shapes[c]
        block = pltpu.VMEM(shape, jnp.bfloat16)
        if kind == "T":
            _, token = call(name, token_kernel, [], (token,), [VMEM], [], token)
        elif kind == "W":
            staged = (mid_w, low_w, out_w)
            (mid_w, low_w, out_w), token = call(name, stage_kernel, [v.shape for v in staged], (token, *staged),
                                                      [VMEM] + [ANY] * 3, [VMEM] * 3, token, scratch_shapes=[DMA((3,))])
        elif kind == "L":
            (field[c],), token = call(name, part(leaf_kernel, first), [shape], (leaf_w, samples, token), [ANY, ANY, VMEM],
                                      [VMEM], token,
                                      scratch_shapes=[block, block, DMA((2,))])
            other[c] = swap(field[c], lvl_bits - 1)
        elif kind == "U" and (step < upper_count - 1 or c < len(WIDTHS) - 1):
            (field[c],), token = call(name, part(level_kernel, first, step), [shape], (up_w, field[c], other[c], token),
                                      [VMEM] * 4, [VMEM], token)
            if step < upper_count - 1:
                other[c] = swap(field[c], lvl_bits - 2 - step)
        elif kind == "U":
            earlier = [field[e] for e in range(c)]
            sends, token = call(name, part(spread_kernel, first, step), [(inner,) + box] * mid_size,
                                (up_w, field[c], other[c], token, *earlier), [VMEM] * (4 + len(earlier)),
                                [VMEM] * mid_size, token)
            got = [across(send, gap) if gap else send for gap, send in enumerate(sends)]
        elif kind == "M":
            gaps = tuple(range(c, mid_size, 2))
            tall = (len(gaps), inner)
            count = PIECES[c]
            fields, token = call(name, part(middle_kernel, gaps, ORDER[c]), [(len(gaps), inner // count) + box] * count,
                                 (mid_w, token, *[got[q] for q in ORDER[c]]), [VMEM] * (2 + len(gaps)), [VMEM] * count,
                                 token, scratch_shapes=[pltpu.VMEM(tall + box, jnp.bfloat16)])
            for piece, value in enumerate(fields):
                e = sum(PIECES[:c]) + piece
                field[e], other[e] = value, swap(value, lower_count - 1)
                place[e] = (gaps, piece * (inner // count))
        elif kind == "D":
            (field[c],), token = call(name, part(lower_kernel, *place[c], step), [field[c].shape],
                                      (low_w, field[c], other[c], token), [VMEM] * 4, [VMEM], token)
            other[c] = swap(field[c], lower_count - 2 - step)
        elif item != PLAN[-1]:
            (done,), token = call(name, part(finish_kernel, *place[c], lower_count - 1), [field[c].shape],
                                  (low_w, out_w, token, field[c], other[c]), [VMEM] * 5, [VMEM], token)
            finished.append(done)
        else:
            args = (low_w, out_w, token, field[c], other[c], *finished)
            places = [place[e] for e in range(c + 1)]
            result = pl.pallas_call(
                part(store_kernel, places, lower_count - 1),
                out_shape=jax.ShapeDtypeStruct(samples.shape, jnp.bfloat16),
                in_specs=[VMEM] * len(args),
                out_specs=ANY,
                scratch_shapes=[pltpu.VMEM(field[c].shape, jnp.bfloat16), DMA((mid_size // 2 * len(places),))],
                compiler_params=pltpu.CompilerParams(vmem_limit_bytes=8 << 20),
                cost_estimate=pl.CostEstimate(flops=1, bytes_accessed=1, transcendentals=0),
            )(*args)
    return result.reshape(signal.shape)


def solution(mesh):
    boxes = P(("lvl", "mid"), None, None)
    levels = P(None, ("lvl", "mid"), None, None)
    return jax.shard_map(
        on_device,
        mesh=mesh,
        in_specs=(boxes, boxes, levels, levels, levels, boxes),
        out_specs=boxes,
        check_vma=False,
    )
```

```python
import functools

import jax
import jax.numpy as jnp
from jax import lax
from jax.experimental import pallas as pl
from jax.experimental.pallas import tpu as pltpu
from jax.sharding import PartitionSpec as P

WIDTHS = (1, 1, 1, 1)
PIECES = (1, 1)
ORDER = ((0, 4, 6, 2), (7, 5, 1, 3))
PLAN = (
    "T0", "L0", "L1", "L2", "L3", "U00", "U01", "U02", "U03", "U10", "U11", "U12", "U13", "U20", "U21",
    "W0", "U22", "U23", "M0", "M1", "D00", "D01", "E0", "E1",
)
VMEM = pl.BlockSpec(memory_space=pltpu.VMEM)
ANY = pl.BlockSpec(memory_space=pl.ANY)
DMA = pltpu.SemaphoreType.DMA
TOKEN = jax.ShapeDtypeStruct((8, 128), jnp.float32)
COST = {"T0": 100}


def turn(piece):
    half = piece.shape[-1] // 2
    rolled = pltpu.roll(piece.astype(jnp.float32), half, 1)
    lane = lax.broadcasted_iota(jnp.int32, piece.shape, 1)
    return jnp.where(lane < half, -rolled, rolled).astype(jnp.bfloat16)


def product(weights, parts, turned=None):
    turned = [turn(p) for p in parts] if turned is None else turned
    stacked = jnp.concatenate(list(parts) + list(turned), axis=0)
    return jnp.dot(weights, stacked, preferred_element_type=jnp.float32).astype(jnp.bfloat16)


def token_kernel(t_ref, u_ref):
    u_ref[...] = t_ref[...]


def leaf_kernel(first, w_ref, x_ref, t_ref, o_ref, u_ref, ws_ref, xs_ref, sems):
    u_ref[...] = t_ref[...]
    width = o_ref.shape[1]
    loads = [
        pltpu.make_async_copy(w_ref.at[:, first:first + width], ws_ref, sems.at[0]),
        pltpu.make_async_copy(x_ref.at[:, first:first + width], xs_ref, sems.at[1]),
    ]
    for load in loads:
        load.start()
    for load in loads:
        load.wait()
    for a in range(o_ref.shape[0]):
        for b in range(width):
            o_ref[a, b] = product(ws_ref[a, b], [xs_ref[a, b]])


def stage_kernel(t_ref, *refs):
    count = (len(refs) - 2) // 2
    u_ref, sems = refs[-2:]
    u_ref[...] = t_ref[...]
    loads = [pltpu.make_async_copy(refs[i], refs[count + i], sems.at[i]) for i in range(count)]
    for load in loads:
        load.start()
    for load in loads:
        load.wait()


def level_kernel(first, step, w_ref, x_ref, y_ref, t_ref, o_ref, u_ref):
    u_ref[...] = t_ref[...]
    for a in range(o_ref.shape[0]):
        for b in range(o_ref.shape[1]):
            o_ref[a, b] = product(w_ref[step, a, first + b], [x_ref[a, b], y_ref[a, b]])


def spread_kernel(first, step, w_ref, x_ref, y_ref, t_ref, *refs):
    *earlier, u_ref = refs
    count = x_ref.shape[0]
    earlier, outs = earlier[:-count], earlier[-count:]
    u_ref[...] = t_ref[...]
    me = lax.axis_index("mid")
    for q in range(count):
        a = me ^ q
        at = 0
        for e_ref in earlier:
            outs[q][at:at + e_ref.shape[1]] = e_ref[a]
            at += e_ref.shape[1]
        for b in range(x_ref.shape[1]):
            outs[q][at + b] = product(w_ref[step, a, first + b], [x_ref[a, b], y_ref[a, b]])


def middle_kernel(gaps, order, w_ref, t_ref, *refs):
    count = len(gaps)
    got = [refs[order.index(q)] for q in gaps]
    outs, u_ref, s_ref = refs[count:-2], refs[-2], refs[-1]
    u_ref[...] = t_ref[...]
    me = lax.axis_index("mid")
    width = outs[0].shape[1]
    for b in range(s_ref.shape[1]):
        for i in range(count // 2):
            pair = (i, i ^ (count // 2))
            parts = {e: got[e][b] for e in pair}
            turned = {e: turn(parts[e]) for e in pair}
            for e in pair:
                order = (e, e ^ (count // 2))
                s_ref[e, b] = product(w_ref[0, me ^ gaps[e], b], [parts[o] for o in order], [turned[o] for o in order])
    for b in range(s_ref.shape[1]):
        for i in range(0, count, 2):
            pair = (i, i ^ (count // 4))
            parts = {e: s_ref[e, b] for e in pair}
            turned = {e: turn(parts[e]) for e in pair}
            for e in pair:
                order = (e, e ^ (count // 4))
                outs[b // width][e, b % width] = product(
                    w_ref[1, me ^ gaps[e], b], [parts[o] for o in order], [turned[o] for o in order]
                )


def lower_kernel(gaps, first, step, w_ref, x_ref, y_ref, t_ref, o_ref, u_ref):
    u_ref[...] = t_ref[...]
    me = lax.axis_index("mid")
    for i, q in enumerate(gaps):
        for b in range(o_ref.shape[1]):
            o_ref[i, b] = product(w_ref[step, me ^ q, first + b], [x_ref[i, b], y_ref[i, b]])


def finish(gaps, first, step, w_ref, v_ref, x_ref, y_ref, r_ref):
    me = lax.axis_index("mid")
    for i, q in enumerate(gaps):
        for b in range(x_ref.shape[1]):
            value = product(w_ref[step, me ^ q, first + b], [x_ref[i, b], y_ref[i, b]])
            r_ref[i, b] = product(v_ref[me ^ q, first + b], [value])


def finish_kernel(gaps, first, step, w_ref, v_ref, t_ref, x_ref, y_ref, r_ref, u_ref):
    u_ref[...] = t_ref[...]
    finish(gaps, first, step, w_ref, v_ref, x_ref, y_ref, r_ref)


def store_kernel(places, step, w_ref, v_ref, t_ref, x_ref, y_ref, *refs):
    *earlier, o_ref, r_ref, sems = refs
    me = lax.axis_index("mid")

    def stores(c, source):
        gaps, first = places[c]
        width = source.shape[1]
        return [
            pltpu.make_async_copy(source.at[i], o_ref.at[me ^ q, first:first + width], sems.at[c * len(gaps) + i])
            for i, q in enumerate(gaps)
        ]

    moving = [store for c, e_ref in enumerate(earlier) for store in stores(c, e_ref)]
    for store in moving:
        store.start()
    gaps, first = places[-1]
    final = stores(len(places) - 1, r_ref)
    for i, q in enumerate(gaps):
        for b in range(x_ref.shape[1]):
            value = product(w_ref[step, me ^ q, first + b], [x_ref[i, b], y_ref[i, b]])
            r_ref[i, b] = product(v_ref[me ^ q, first + b], [value])
        final[i].start()
    for store in moving + final:
        store.wait()


def call(kind, kernel, shapes, args, specs, out_specs, token, **kw):
    *outs, token = pl.pallas_call(
        kernel,
        out_shape=[jax.ShapeDtypeStruct(shape, jnp.bfloat16) for shape in shapes] + [TOKEN],
        in_specs=specs,
        out_specs=list(out_specs) + [VMEM],
        compiler_params=pltpu.CompilerParams(vmem_limit_bytes=8 << 20),
        cost_estimate=pl.CostEstimate(flops=1 + int(COST.get(kind, 0) * 1e9), bytes_accessed=1, transcendentals=0),
        **kw,
    )(*args)
    return outs, token


def on_device(signal, leaf_in, upper_w, middle_w, lower_w, leaf_out):
    lvl_size, mid_size = lax.axis_size("lvl"), lax.axis_size("mid")
    lvl_bits = lvl_size.bit_length() - 1
    inner = signal.shape[0] // mid_size
    box = signal.shape[1:]
    part = functools.partial
    leaf_w, up_w, mid_w, low_w, out_w, samples = (
        v.reshape(v.shape[:-3] + (mid_size, inner) + v.shape[-2:])
        for v in (leaf_in, upper_w, middle_w, lower_w, leaf_out, signal)
    )
    firsts = [sum(WIDTHS[:c]) for c in range(len(WIDTHS))]
    shapes = [(mid_size, w) + box for w in WIDTHS]

    def swap(block, bit):
        return lax.ppermute(block, "lvl", [(i, i ^ (1 << bit)) for i in range(lvl_size)])

    def across(block, gap):
        return lax.ppermute(block, "mid", [(i, i ^ gap) for i in range(mid_size)])

    field, other, place = {}, {}, {}
    token = jnp.zeros(TOKEN.shape, TOKEN.dtype)
    result, finished = None, []
    lower_count = lower_w.shape[0]
    upper_count = upper_w.shape[0]
    for item in PLAN:
        kind, c = item[0], int(item[-1])
        step = int(item[1])
        name = item
        first, shape = firsts[c], shapes[c]
        block = pltpu.VMEM(shape, jnp.bfloat16)
        if kind == "T":
            _, token = call(name, token_kernel, [], (token,), [VMEM], [], token)
        elif kind == "W":
            staged = (mid_w, low_w, out_w)
            (mid_w, low_w, out_w), token = call(name, stage_kernel, [v.shape for v in staged], (token, *staged),
                                                      [VMEM] + [ANY] * 3, [VMEM] * 3, token, scratch_shapes=[DMA((3,))])
        elif kind == "L":
            (field[c],), token = call(name, part(leaf_kernel, first), [shape], (leaf_w, samples, token), [ANY, ANY, VMEM],
                                      [VMEM], token,
                                      scratch_shapes=[block, block, DMA((2,))])
            other[c] = swap(field[c], lvl_bits - 1)
        elif kind == "U" and (step < upper_count - 1 or c < len(WIDTHS) - 1):
            (field[c],), token = call(name, part(level_kernel, first, step), [shape], (up_w, field[c], other[c], token),
                                      [VMEM] * 4, [VMEM], token)
            if step < upper_count - 1:
                other[c] = swap(field[c], lvl_bits - 2 - step)
        elif kind == "U":
            earlier = [field[e] for e in range(c)]
            sends, token = call(name, part(spread_kernel, first, step), [(inner,) + box] * mid_size,
                                (up_w, field[c], other[c], token, *earlier), [VMEM] * (4 + len(earlier)),
                                [VMEM] * mid_size, token)
            got = [across(send, gap) if gap else send for gap, send in enumerate(sends)]
        elif kind == "M":
            gaps = tuple(range(c, mid_size, 2))
            tall = (len(gaps), inner)
            count = PIECES[c]
            fields, token = call(name, part(middle_kernel, gaps, ORDER[c]), [(len(gaps), inner // count) + box] * count,
                                 (mid_w, token, *[got[q] for q in ORDER[c]]), [VMEM] * (2 + len(gaps)), [VMEM] * count,
                                 token, scratch_shapes=[pltpu.VMEM(tall + box, jnp.bfloat16)])
            for piece, value in enumerate(fields):
                e = sum(PIECES[:c]) + piece
                field[e], other[e] = value, swap(value, lower_count - 1)
                place[e] = (gaps, piece * (inner // count))
        elif kind == "D":
            (field[c],), token = call(name, part(lower_kernel, *place[c], step), [field[c].shape],
                                      (low_w, field[c], other[c], token), [VMEM] * 4, [VMEM], token)
            other[c] = swap(field[c], lower_count - 2 - step)
        elif item != PLAN[-1]:
            (done,), token = call(name, part(finish_kernel, *place[c], lower_count - 1), [field[c].shape],
                                  (low_w, out_w, token, field[c], other[c]), [VMEM] * 5, [VMEM], token)
            finished.append(done)
        else:
            args = (low_w, out_w, token, field[c], other[c], *finished)
            places = [place[e] for e in range(c + 1)]
            result = pl.pallas_call(
                part(store_kernel, places, lower_count - 1),
                out_shape=jax.ShapeDtypeStruct(samples.shape, jnp.bfloat16),
                in_specs=[VMEM] * len(args),
                out_specs=ANY,
                scratch_shapes=[pltpu.VMEM(field[c].shape, jnp.bfloat16), DMA((mid_size // 2 * len(places),))],
                compiler_params=pltpu.CompilerParams(vmem_limit_bytes=8 << 20),
                cost_estimate=pl.CostEstimate(flops=1, bytes_accessed=1, transcendentals=0),
            )(*args)
    return result.reshape(signal.shape)


def solution(mesh):
    boxes = P(("lvl", "mid"), None, None)
    levels = P(None, ("lvl", "mid"), None, None)
    return jax.shard_map(
        on_device,
        mesh=mesh,
        in_specs=(boxes, boxes, levels, levels, levels, boxes),
        out_specs=boxes,
        check_vma=False,
    )
```
